32 devices in a mesh: ptg: 4 (over z), img: 8 (over y, x, core).
Axes of the slice: x: 2, y: 2, z: 4, core: 2. Of those that a mesh axis runs over, the one named last changes fastest.
Arguments:
- image: bfloat16 [2048, 4096], P(None, 'img'), may hold values from -6 to 6
- beam: float32 [4, 2048, 2048], P('ptg', 'img'), may hold values from 0.2 to 1
- counts: int32 [4, 2048, 2048], P('ptg', None, 'img'), may hold values from 0 to 15
- offsets: int32 [4], P('ptg'), may hold values from 0 to 2048, as said below
Outputs:
- hessian_image: float32 [2048, 4096], P('ptg', 'img')
The draws below stay inside these ranges and needn't reach their ends.
Inputs may be any that keep to these rules, and one draw needn't show every extreme that they name: offsets rise with the pointing; the first is 0 and the last is 2048.
All inputs are finite; a program needn't handle non-finite values.
Results may differ from the reference program's by a relative error of at most 0.0095.
Values may be sent and summed in bfloat16 or wider, within the bound.
A program may use at most 64 MiB of HBM per device.

```python
import math
import jax
import jax.numpy as jnp
from jax import lax

POINT = 2048
NPTG = 4
WIDTH = 4096


def draw_offsets(key, part):
    key = jax.random.fold_in(key, 5)
    span = WIDTH - POINT
    index_ptg = jnp.arange(NPTG, dtype=jnp.int32)
    base = index_ptg * span // (NPTG - 1)
    reach = span // (4 * (NPTG - 1))
    jitter = jax.random.randint(key, (NPTG,), -reach, reach + 1, dtype=jnp.int32)
    inner = (index_ptg > 0) & (index_ptg < NPTG - 1)
    return jnp.clip(base + jnp.where(inner, jitter, 0), 0, span).astype(jnp.int32)


def set_ends(entries, own_key, least, largest):
    extent = entries.shape
    place = [jax.random.randint(jax.random.fold_in(own_key, axis), (), 0, extent[axis]) for axis in range(len(extent))]
    entries = entries.at[tuple(place)].set(least)
    longest = extent.index(max(extent))
    place[longest] = (place[longest] + 1) % extent[longest]
    return entries.at[tuple(place)].set(largest)


def level_of(key, dims, split, least, high):
    def one(dim, shards_of):
        heights = jax.random.uniform(jax.random.fold_in(jax.random.fold_in(key, 6), dim), (shards_of,), jnp.float32, least / len(split), high / len(split))
        return jnp.repeat(jnp.exp(heights), dims[dim] // shards_of).reshape((-1,) + (1,) * (len(dims) - dim - 1))

    gain = one(*split[0])
    for cut in split[1:]:
        gain = gain * one(*cut)
    return gain


def noise(stream_key, extent, spread, bound, split=(), held_as=jnp.bfloat16):
    gain = level_of(stream_key, extent, split, -0.22, 0.18) if split else 1.0
    values = jax.random.normal(stream_key, extent, jnp.float32) * spread * gain
    return jnp.minimum(jnp.maximum(values, -bound), bound).astype(held_as)


def setup_inputs(seed: int = 0) -> dict:
    key_list = jax.random.split(jax.random.key(seed), 5)
    image = noise(key_list[0], (POINT, WIDTH), 1.0, 6.0, ((1, 8),))
    beam = jnp.clip(0.2 + 0.8 * jax.random.uniform(key_list[1], (NPTG, POINT, POINT), jnp.float32) ** level_of(key_list[1], (NPTG, POINT, POINT), ((0, 4), (1, 8)), -0.2, 0.2), 0.2, 1.0)
    counts = set_ends(jax.random.randint(key_list[2], (NPTG, POINT, POINT), 0, 16), jax.random.fold_in(key_list[2], 1), 0, 15).astype(jnp.int32)
    offsets = draw_offsets(jax.random.fold_in(key_list[4], 71), 0)
    return {"image": image, "beam": beam, "counts": counts, "offsets": offsets}


def tables(points):
    index_row = jnp.arange(points, dtype=jnp.int32)
    phase = (index_row[:, None] * index_row[None, :]) % points
    angle = phase.astype(jnp.float32) * (2.0 * math.pi / points)
    return jnp.cos(angle).astype(jnp.bfloat16), (-jnp.sin(angle)).astype(jnp.bfloat16)


def reference(image, beam, counts, offsets):
    cosine, sine_table = tables(POINT)
    total = jnp.zeros((POINT, WIDTH), jnp.float32)
    for pointing in range(NPTG):
        start = offsets[pointing].astype(jnp.int32)
        window = lax.dynamic_slice_in_dim(image, start, POINT, 1)
        beamed = (beam[pointing] * window.astype(jnp.float32)).astype(jnp.bfloat16)
        row_real = jnp.dot(beamed, cosine, preferred_element_type=jnp.float32).astype(jnp.bfloat16)
        row_imag = jnp.dot(beamed, sine_table, preferred_element_type=jnp.float32).astype(jnp.bfloat16)
        spec_real = jnp.dot(cosine, row_real, preferred_element_type=jnp.float32) - jnp.dot(sine_table, row_imag, preferred_element_type=jnp.float32)
        spec_imag = jnp.dot(sine_table, row_real, preferred_element_type=jnp.float32) + jnp.dot(cosine, row_imag, preferred_element_type=jnp.float32)
        weight = counts[pointing].astype(jnp.float32) / float(POINT * POINT)
        weighted_real = (weight * spec_real).astype(jnp.bfloat16)
        weighted_imag = (weight * spec_imag).astype(jnp.bfloat16)
        back_real = (jnp.dot(cosine, weighted_real, preferred_element_type=jnp.float32) + jnp.dot(sine_table, weighted_imag, preferred_element_type=jnp.float32)).astype(jnp.bfloat16)
        back_imag = (jnp.dot(cosine, weighted_imag, preferred_element_type=jnp.float32) - jnp.dot(sine_table, weighted_real, preferred_element_type=jnp.float32)).astype(jnp.bfloat16)
        image_real = jnp.dot(back_real, cosine, preferred_element_type=jnp.float32) + jnp.dot(back_imag, sine_table, preferred_element_type=jnp.float32)
        contribution = (beam[pointing] * image_real).astype(jnp.bfloat16)
        current = lax.dynamic_slice_in_dim(total, start, POINT, 1)
        total = lax.dynamic_update_slice_in_dim(total, current + contribution.astype(jnp.float32), start, 1)
    return total
```

```python
import jax
import jax.numpy as jnp
import ml_dtypes
import numpy as np
from jax import lax
from jax.sharding import PartitionSpec as P

BF = ml_dtypes.bfloat16


def slots_of(points, parts):
    wide = points // parts
    half = wide // 2
    rows = []
    for d in range(parts):
        first = wide * d + (0 if d < parts // 2 else 1)
        rows.append(np.arange(first, first + half))
    return np.stack(rows)


def make_tables(points, parts):
    index = np.arange(points, dtype=np.int64)
    angle = 2.0 * np.pi / points * np.arange(points)
    cos_of, sin_of = np.cos(angle), -np.sin(angle)
    phase = index[:, None] * index[None, :] % points
    column = np.concatenate([cos_of[phase], sin_of[phase]], 0).astype(BF)
    slots = slots_of(points, parts)
    blocks = []
    for d in range(parts):
        phase = index[:, None] * slots[d][None, :] % points
        real, imag = cos_of[phase], sin_of[phase]
        if d == 0:
            imag[:, 0] = 1.0 - 2.0 * (index % 2)
        blocks += [real, imag]
    return column, np.concatenate(blocks, 1).astype(BF)


def make_selectors(points, parts):
    wide = points // parts
    half = wide // 2
    send = np.zeros((parts, wide, half), BF)
    own = np.zeros((parts, wide, wide), BF)
    mirror_own = np.zeros((parts, wide, wide), BF)
    mirror_recv = np.zeros((parts, half, wide), BF)
    mirror_col = np.zeros((parts, 8, wide), BF)
    own_col = np.zeros((parts, 8, wide), BF)
    scale = np.full((parts, 1, wide), 1.0 / float(points * points), np.float32)
    for d in range(parts):
        low = d < parts // 2
        for j in range(half):
            if low:
                send[d, wide - 1 - j, j] = 1
                own[d, j, j] = own[d, j, half + j] = 1
            else:
                if j:
                    send[d, wide - j, j] = 1
                own[d, j + 1, j] = own[d, j + 1, half + j] = 1
            if j or not low:
                mirror_recv[d, j, j] = mirror_recv[d, j, half + j] = 1
        if d == 0:
            own[d, 0, half] = 0
            mirror_own[d, 0, 0] = 1
            own_col[d, 0, half] = mirror_col[d, 0, half] = 1
            scale[d, 0, 0] = scale[d, 0, half] = 0.5 / float(points * points)
        elif low:
            mirror_col[d, 0, 0] = mirror_col[d, 0, half] = 1
    return send, own, mirror_own, mirror_recv, mirror_col, own_col, scale


def dot(a, b, dims=((1,), (0,))):
    return lax.dot_general(a, b, (dims, ((), ())), preferred_element_type=jnp.float32)


def weights(counts, points, parts):
    me = lax.axis_index("img")
    send, own, mirror_own, mirror_recv, mirror_col, own_col, scale = (
        jnp.asarray(a)[me] for a in make_selectors(points, parts)
    )
    values = counts.astype(jnp.bfloat16)
    sent = dot(values, send).astype(jnp.bfloat16)
    pairs = [(d, parts - 1 - d) for d in range(parts)]
    recv = lax.ppermute(sent, "img", pairs)
    first = np.zeros((8, points // parts), BF)
    first[0, 0] = 1
    column = dot(jnp.asarray(first), values, ((1,), (1,))).astype(jnp.bfloat16)
    pairs = [(parts // 2, 0)] + [(parts - d, d) for d in range(1, parts // 2)]
    column = lax.ppermute(column, "img", pairs)
    mirror = dot(recv, mirror_recv) + dot(values, mirror_own) + dot(column, mirror_col, ((0,), (0,)))
    index = jnp.arange(points, dtype=jnp.int32)
    flip = ((index[:, None] + index[None, :]) % points == 0).astype(jnp.bfloat16)
    total = dot(values, own) + dot(column, own_col, ((0,), (0,))) + dot(flip, mirror.astype(jnp.bfloat16))
    return total * scale


def shards(image, beam, counts, offsets):
    points = counts.shape[1]
    parts, layers = lax.axis_size("img"), lax.axis_size("ptg")
    me, layer = lax.axis_index("img"), lax.axis_index("ptg")
    tile = image.shape[1]
    folds = tile * parts // points
    rows = points // parts
    wide, half = points // parts, points // parts // 2
    chunk = points // layers
    start = offsets[0]
    table_np, row_np = make_tables(points, parts)
    table, row_table = jnp.asarray(table_np), jnp.asarray(row_np)

    strip = lax.all_to_all(image, "img", split_axis=0, concat_axis=1, tiled=True)
    starts = lax.all_gather(offsets, "ptg", tiled=True)
    weight = weights(counts[0], points, parts)
    shift = start % points
    twice = jnp.concatenate([beam[0], beam[0]], 1)
    rolled = lax.dynamic_slice_in_dim(twice, points - shift, points, 1)

    place = jnp.arange(points, dtype=jnp.int32)
    window = strip[:, (folds - 1) * points :]
    for f in range(folds - 2, -1, -1):
        window = jnp.where(place + f * points >= start, strip[:, f * points : (f + 1) * points], window)
    beamed = (rolled * window.astype(jnp.float32)).astype(jnp.bfloat16)
    row = dot(beamed, row_table).astype(jnp.bfloat16)
    col = lax.all_to_all(row, "img", split_axis=1, concat_axis=0, tiled=True)
    spec = dot(table, col)
    c_re, c_im = spec[:points, :half], spec[:points, half:]
    s_re, s_im = spec[points:, :half], spec[points:, half:]
    packed = (jnp.arange(half) == 0) & (me == 0)
    real, imag = c_re - s_im, s_re + c_im
    upper = jnp.concatenate([jnp.where(packed, c_re, real), jnp.where(packed, c_im, imag)], 1)
    lower = jnp.concatenate([jnp.where(packed, s_re, imag), jnp.where(packed, s_im, -real)], 1)
    weighted = jnp.concatenate([weight * upper, weight * lower], 0).astype(jnp.bfloat16)
    back = dot(table, weighted, ((0,), (0,))).astype(jnp.bfloat16)
    rows_back = lax.all_to_all(back, "img", split_axis=0, concat_axis=1, tiled=True)
    contribution = (rolled * dot(rows_back, row_table, ((1,), (1,)))).astype(jnp.bfloat16)
    terms = lax.all_to_all(contribution, "ptg", split_axis=1, concat_axis=0, tiled=True)
    terms = terms.reshape(layers, rows, chunk).astype(jnp.float32)

    at = layer * chunk + jnp.arange(chunk, dtype=jnp.int32)
    sums = []
    for f in range(folds):
        inside = (at + f * points >= starts[:, None]) & (at + f * points < starts[:, None] + points)
        sums.append(jnp.sum(jnp.where(inside[:, None, :], terms, 0.0), 0).astype(jnp.bfloat16))
    sums = jnp.stack(sums)

    out_rows = points // layers
    tall, broad = out_rows // rows, tile // chunk
    out = jnp.zeros((out_rows, tile), jnp.float32)
    for s in range(folds):
        pairs = []
        row_at = np.zeros((layers * parts,), np.int32)
        col_at = np.zeros((layers * parts,), np.int32)
        for p in range(layers):
            for i in range(parts):
                f = (i % tall * broad + p % broad + s) % folds
                q, c = i * rows // out_rows, (points * f + chunk * p) // tile
                pairs.append((p * parts + i, q * parts + c))
                row_at[q * parts + c] = i * rows - q * out_rows
                col_at[q * parts + c] = points * f + chunk * p - tile * c
        piece = lax.dynamic_index_in_dim(sums, (me % tall * broad + layer % broad + s) % folds, 0, False)
        piece = lax.ppermute(piece, ("ptg", "img"), pairs)
        here = layer * parts + me
        out = lax.dynamic_update_slice(
            out, piece.astype(jnp.float32), (jnp.asarray(row_at)[here], jnp.asarray(col_at)[here])
        )
    return out


def solution(mesh):
    return jax.shard_map(
        shards,
        mesh=mesh,
        in_specs=(P(None, "img"), P("ptg", "img", None), P("ptg", None, "img"), P("ptg")),
        out_specs=P("ptg", "img"),
        check_vma=False,
    )
```

```python
import jax
import jax.numpy as jnp
import numpy as np
from jax import lax
from jax.experimental import pallas as pl
from jax.experimental.pallas import tpu as pltpu
from jax.sharding import PartitionSpec as P


def make_tables(points):
    angle = 2.0 * np.pi / points * np.arange(points)
    cos_of, sin_of = np.cos(angle), -np.sin(angle)
    index = np.arange(points, dtype=np.int64)
    coarse = index[::8, None] * index[None, :] % points
    fine = index[:8, None] * index[None, :] % points
    return [t[p].astype(np.float32) for p in (coarse, fine) for t in (cos_of, sin_of)]


MESH = pl.DeviceIdType.MESH
BLOCK = 256


def dot(a, b, dims=((1,), (0,))):
    return lax.dot_general(a, b, (dims, ((), ())), preferred_element_type=jnp.float32)


def remote(src, dst, send, recv, device):
    return pltpu.make_async_remote_copy(
        src_ref=src, dst_ref=dst, send_sem=send, recv_sem=recv, device_id=device, device_id_type=MESH
    )


def arrived(ref, sem):
    pltpu.make_async_copy(ref, ref, sem).wait()


def kernel(
    image, beam_hbm, counts_hbm, start, coarse_cos_hbm, coarse_sin_hbm, fine_cos, fine_sin,
    sums,
    column, coarse_cos, coarse_sin, beam, counts, strip, beamed, row_out, col_in, weighted, back_out, back_in,
    real_in, imag_in, given, terms, starts, values, weight, sent, recv, mirror, first_out, first_in,
    load_sem, own_sem, image_send, image_recv, row_send, row_recv, back_send, back_recv,
    layer_send, layer_recv, start_send, start_recv, count_sem,
):
    parts, rows, tile = strip.shape
    layers, _, chunk = terms.shape
    folds = sums.shape[0]
    points = rows * parts
    wide = counts.shape[1]
    half = wide // 2
    me, layer = lax.axis_index("img"), lax.axis_index("ptg")

    def peer(k):
        return lax.rem(me + k, parts)

    def above(k):
        return lax.rem(layer + k, layers)

    def rows_of(d):
        return pl.ds(pl.multiple_of(d * rows, rows), rows)

    loads = [
        pltpu.make_async_copy(src, dst, load_sem.at[at])
        for at, (src, dst) in enumerate(
            [(counts_hbm, counts), (coarse_cos_hbm, coarse_cos), (coarse_sin_hbm, coarse_sin), (beam_hbm, beam)]
        )
    ]
    mine = pltpu.make_async_copy(image.at[rows_of(me), :], strip.at[me], own_sem)
    mine.start()
    for load in loads:
        load.start()

    barrier = pltpu.get_barrier_semaphore()
    for k in range(1, parts):
        pl.semaphore_signal(barrier, inc=1, device_id=(layer, peer(k)), device_id_type=MESH)
    for k in range(1, layers):
        pl.semaphore_signal(barrier, inc=1, device_id=(above(k), me), device_id_type=MESH)
    pl.semaphore_wait(barrier, parts + layers - 2)

    def image_copy(k):
        d = peer(k)
        return remote(image.at[rows_of(d), :], strip.at[me], image_send.at[k], image_recv.at[me], (layer, d))

    def start_copy(k):
        return remote(start, starts.at[layer], start_send.at[k], start_recv.at[layer], (above(k), me))

    for k in range(1, parts):
        image_copy(k).start()
    for k in range(1, layers):
        start_copy(k).start()
    starts[layer] = start[...]

    low = me < parts // 2

    def grid(shape):
        return lax.broadcasted_iota(jnp.int32, shape, 0), lax.broadcasted_iota(jnp.int32, shape, 1)

    def ones(where):
        return jnp.where(where, 1.0, 0.0).astype(jnp.bfloat16)

    def at_low(where):
        return jnp.logical_and(where, low)

    def at_high(where):
        return jnp.logical_and(where, jnp.logical_not(low))

    def at_first(where):
        return jnp.logical_and(where, me == 0)

    loads[0].wait()
    values[...] = counts[...].astype(jnp.float32).astype(jnp.bfloat16)
    i, j = grid((wide, sent.shape[1]))
    sel = at_low((i == half + j) & (j < half)) | at_high((i == wide - j) & (j >= 1) & (j < half))
    sent[...] = dot(values[...], ones(sel)).astype(jnp.bfloat16)
    i, j = grid((16, wide))
    first_out[...] = dot(ones(i + j == 0), values[...], ((1,), (1,))).astype(jnp.bfloat16)
    other = lax.rem(parts - me, parts)
    other = jnp.where(me == 0, parts // 2, jnp.where(me == parts // 2, 0, other))
    count_copy = remote(sent, recv, count_sem.at[0], count_sem.at[1], (layer, parts - 1 - me))
    first_copy = remote(first_out, first_in, count_sem.at[2], count_sem.at[3], (layer, other))
    count_copy.start()
    first_copy.start()

    loads[1].wait()
    loads[2].wait()

    @pl.loop(0, points // 64)
    def _(g):
        eight = pl.ds(pl.multiple_of(g * 8, 8), 8)
        for c in range(0, points, 256):
            at = pl.ds(c, 256)
            cos_a, sin_a = coarse_cos[eight, at], coarse_sin[eight, at]
            cos_b, sin_b = fine_cos[:, at], fine_sin[:, at]
            for r in range(0, 8, 2):
                cos_rows, sin_rows = [], []
                for t in (r, r + 1):
                    cos_t, sin_t = cos_a[t : t + 1], sin_a[t : t + 1]
                    cos_rows.append(cos_t * cos_b - sin_t * sin_b)
                    sin_rows.append(sin_t * cos_b + cos_t * sin_b)
                to = pl.multiple_of(g * 64 + r * 8, 16)
                column[pl.ds(to, 16), at] = jnp.concatenate(cos_rows, 0).astype(jnp.bfloat16)
                column[pl.ds(points + to, 16), at] = jnp.concatenate(sin_rows, 0).astype(jnp.bfloat16)

    loads[3].wait()
    mine.wait()
    origin = start[0:1, 0:1]
    per_fold = points // tile
    for t in range(per_fold):
        for f in range(folds):
            src = t + per_fold * f

            @pl.when(src != me)
            def _():
                arrived(strip.at[src], image_recv.at[src])

        place = lax.broadcasted_iota(jnp.int32, (rows, tile), 1) + t * tile
        window = strip[t + per_fold * (folds - 1)].astype(jnp.float32)
        for f in range(folds - 2, -1, -1):
            window = jnp.where(place + f * points >= origin, strip[t + per_fold * f].astype(jnp.float32), window)
        at = pl.ds(t * tile, tile)
        beamed[:, at] = (beam[:, at] * window).astype(jnp.bfloat16)

    def columns_of(d):
        return pl.ds(pl.multiple_of(d * wide, wide), wide)

    def row_copy(d):
        return remote(row_out.at[d], col_in.at[rows_of(me), :], row_send.at[d], row_recv.at[me], (layer, d))

    _, j = grid((rows, points))
    sides = jnp.where(lax.rem(j, 2) == 0, beamed[...].astype(jnp.float32), -beamed[...].astype(jnp.float32))
    alternating = jnp.sum(sides, 1, keepdims=True)
    _, lane = grid((rows, wide))

    @pl.loop(0, parts // 2)
    def _(step):
        d = lax.rem(me + 1 + step, parts // 2)
        real = dot(beamed[...], column[:points, columns_of(d)])
        imag = dot(beamed[...], column[points:, columns_of(d)])
        imag = jnp.where(jnp.logical_and(lane == 0, d == 0), alternating, imag)
        lower = jnp.where(lane < half, real, pltpu.roll(imag, half, 1)).astype(jnp.bfloat16)
        upper = jnp.where(lane < half, pltpu.roll(real, half, 1), imag).astype(jnp.bfloat16)
        for to, block in ((d, lower), (parts - 1 - d, upper)):

            @pl.when(to == me)
            def _():
                col_in[rows_of(me), :] = block

            @pl.when(to != me)
            def _():
                row_out[to] = block
                row_copy(to).start()

    count_copy.wait()
    first_copy.wait()
    steps = points // BLOCK

    def block_of(b):
        return pl.ds(pl.multiple_of(b * BLOCK, BLOCK), BLOCK)

    i, j = grid((wide, wide))
    own = jnp.logical_and(
        at_low(i == lax.rem(j, half)) | at_high(i == half - lax.rem(j, half)),
        jnp.logical_not(at_first(j == half)),
    )
    own_a, own_b = ones(at_low(own)), ones(at_high(own) | at_first(i + j == 0))
    i, j = grid((recv.shape[1], wide))
    expand = i == lax.rem(j, half)
    recv_a, recv_b = ones(at_high(expand)), ones(at_low(expand))
    i, j = grid((16, wide))
    packed = at_first((i == 0) & (j == half))
    first_a, first_b = ones(packed), ones(packed | at_low((i == 0) & (lax.rem(j, half) == 0) & (me != 0)))
    i, j = grid((BLOCK, BLOCK))
    flip, flip_first = ones(i + j == BLOCK), ones(i + j == 0)
    _, j = grid((1, wide))
    packed = at_first(lax.rem(j, half) == 0)
    scale_row = jnp.where(packed, 0.5, 1.0) * (1.0 / float(points * points))
    sign = jnp.where(packed, 0.0, jnp.where(j < half, -1.0, 1.0))

    mirror[...] = dot(first_in[...], first_b, ((0,), (0,))).astype(jnp.bfloat16)
    weight[...] = dot(first_in[...], first_a, ((0,), (0,))).astype(jnp.bfloat16)

    @pl.loop(0, steps)
    def _(b):
        at = block_of(b)
        total = dot(recv[at, :], recv_b) + dot(values[at, :], own_b)
        mirror[at, :] = (mirror[at, :].astype(jnp.float32) + total).astype(jnp.bfloat16)

    @pl.loop(0, steps)
    def _(b):
        at = block_of(b)
        total = dot(flip, mirror[block_of(steps - 1 - b), :])
        total += dot(flip_first, mirror[block_of(lax.rem(steps - b, steps)), :])
        total += dot(values[at, :], own_a) + dot(recv[at, :], recv_a)
        weight[at, :] = ((weight[at, :].astype(jnp.float32) + total) * scale_row).astype(jnp.bfloat16)

    for k in range(1, parts):
        src = lax.rem(me + parts - k, parts)
        arrived(col_in.at[rows_of(src), :], row_recv.at[src])

    @pl.loop(0, steps)
    def _(b):
        at = block_of(b)
        low = block_of(b + steps)
        cos_part = dot(column[at, :], col_in[...])
        sin_part = dot(column[low, :], col_in[...])
        scale = weight[at, :].astype(jnp.float32)
        weighted[at, :] = (scale * (cos_part + sign * pltpu.roll(sin_part, half, 1))).astype(jnp.bfloat16)
        weighted[low, :] = (scale * (sin_part - sign * pltpu.roll(cos_part, half, 1))).astype(jnp.bfloat16)

    def inverse(d):
        upper = dot(column[rows_of(d), :], weighted[:points, :])
        lower = dot(column[rows_of(d + parts), :], weighted[points:, :])
        return (upper + lower).astype(jnp.bfloat16)

    def back_copy(k):
        d = peer(k)
        return remote(back_out.at[d], back_in.at[me], back_send.at[k], back_recv.at[me], (layer, d))

    @pl.loop(1, parts)
    def _(k):
        d = peer(k)
        back_out[d] = inverse(d)
        back_copy(k).start()

    back_in[me] = inverse(me)
    for k in range(1, parts):
        src = lax.rem(me + parts - k, parts)
        arrived(back_in.at[src], back_recv.at[src])
    for d in range(parts // 2):
        lower = back_in[d].astype(jnp.float32)
        upper = back_in[parts - 1 - d].astype(jnp.float32)
        at = pl.ds(d * wide, wide)
        real_in[:, at] = jnp.where(lane < half, lower, pltpu.roll(upper, half, 1)).astype(jnp.bfloat16)
        imag_in[:, at] = jnp.where(lane < half, pltpu.roll(lower, half, 1), upper).astype(jnp.bfloat16)

    def chunk_of(q):
        return pl.ds(pl.multiple_of(q * chunk, chunk), chunk)

    def contribution(q):
        pixels = dot(real_in[...], column[: points // 2, chunk_of(q)])
        pixels += dot(imag_in[...], column[points : points + points // 2, chunk_of(q)])
        middle = imag_in[:, 0:1].astype(jnp.float32)
        _, at = grid((rows, chunk))
        pixels += jnp.where(lax.rem(at, 2) == 0, middle, -middle)
        return (beam[:, chunk_of(q)] * pixels).astype(jnp.bfloat16)

    def layer_copy(k):
        q = above(k)
        return remote(given.at[q], terms.at[layer], layer_send.at[k], layer_recv.at[layer], (q, me))

    @pl.loop(1, layers)
    def _(k):
        q = above(k)
        given[q] = contribution(q)
        layer_copy(k).start()

    terms[layer] = contribution(layer)
    for k in range(1, layers):
        src = lax.rem(layer + layers - k, layers)
        arrived(starts.at[src], start_recv.at[src])
        arrived(terms.at[src], layer_recv.at[src])

    place = lax.broadcasted_iota(jnp.int32, (rows, chunk), 1) + layer * chunk
    for f in range(folds):
        total = jnp.zeros((rows, chunk), jnp.float32)
        for p in range(layers):
            offset = place + f * points - starts[p][0:1, 0:1]
            inside = (offset >= 0) & (offset < points)
            total += jnp.where(inside, terms[p].astype(jnp.float32), 0.0)
        sums[f] = total.astype(jnp.bfloat16)

    for k in range(1, parts):
        image_copy(k).wait_send()
        back_copy(k).wait_send()
        row_copy(peer(k)).wait_send()
    for k in range(1, layers):
        start_copy(k).wait_send()
        layer_copy(k).wait_send()


def strips(image, beam, counts, start, layers):
    points, wide = counts.shape
    rows, tile = beam.shape[0], image.shape[1]
    parts = points // rows
    folds = tile * parts // points
    chunk = points // layers
    coarse_cos, coarse_sin, fine_cos, fine_sin = (jnp.asarray(t) for t in make_tables(points))
    hp = max(wide // 2, 128)
    vmem, hbm = pl.BlockSpec(memory_space=pltpu.VMEM), pl.BlockSpec(memory_space=pl.ANY)
    bf = jnp.bfloat16
    dma = pltpu.SemaphoreType.DMA
    return pl.pallas_call(
        kernel,
        out_shape=jax.ShapeDtypeStruct((folds, rows, chunk), bf),
        in_specs=[hbm, hbm, hbm, vmem, hbm, hbm, vmem, vmem],
        out_specs=vmem,
        scratch_shapes=[
            pltpu.VMEM((2 * points, points), bf),
            pltpu.VMEM((points // 8, points), jnp.float32),
            pltpu.VMEM((points // 8, points), jnp.float32),
            pltpu.VMEM((rows, points), jnp.float32),
            pltpu.VMEM((points, wide), jnp.int32),
            pltpu.VMEM((parts, rows, tile), bf),
            pltpu.VMEM((rows, points), bf),
            pltpu.VMEM((parts, rows, wide), bf),
            pltpu.VMEM((points, wide), bf),
            pltpu.VMEM((2 * points, wide), bf),
            pltpu.VMEM((parts, rows, wide), bf),
            pltpu.VMEM((parts, rows, wide), bf),
            pltpu.VMEM((rows, points // 2), bf),
            pltpu.VMEM((rows, points // 2), bf),
            pltpu.VMEM((layers, rows, chunk), bf),
            pltpu.VMEM((layers, rows, chunk), bf),
            pltpu.VMEM((layers, 8, 128), jnp.int32),
            pltpu.VMEM((points, wide), bf),
            pltpu.VMEM((points, wide), bf),
            pltpu.VMEM((points, hp), bf),
            pltpu.VMEM((points, hp), bf),
            pltpu.VMEM((points, wide), bf),
            pltpu.VMEM((16, points), bf),
            pltpu.VMEM((16, points), bf),
            dma((4,)), dma(()), dma((parts,)), dma((parts,)), dma((parts,)), dma((parts,)),
            dma((parts,)), dma((parts,)), dma((layers,)), dma((layers,)), dma((layers,)), dma((layers,)),
            dma((4,)),
        ],
        compiler_params=pltpu.CompilerParams(
            collective_id=0, has_side_effects=True, vmem_limit_bytes=60 * 1024 * 1024
        ),
    )(image, beam, counts, start, coarse_cos, coarse_sin, fine_cos, fine_sin)


def shards(image, beam, counts, offsets):
    points = counts.shape[1]
    parts, layers = lax.axis_size("img"), lax.axis_size("ptg")
    me, layer = lax.axis_index("img"), lax.axis_index("ptg")
    tile = image.shape[1]
    folds = tile * parts // points
    rows = points // parts
    chunk = points // layers
    start = offsets[0]
    twice = jnp.concatenate([beam[0], beam[0]], 1)
    rolled = lax.dynamic_slice_in_dim(twice, points - start % points, points, 1)
    sums = strips(image, rolled, counts[0], jnp.full((8, 128), start, jnp.int32), layers)

    out_rows = points // layers
    tall, broad = out_rows // rows, tile // chunk
    out = jnp.zeros((out_rows, tile), jnp.float32)
    for s in range(folds):
        pairs = []
        row_at = np.zeros((layers * parts,), np.int32)
        col_at = np.zeros((layers * parts,), np.int32)
        for p in range(layers):
            for i in range(parts):
                f = (i % tall * broad + p % broad + s) % folds
                q, c = i * rows // out_rows, (points * f + chunk * p) // tile
                pairs.append((p * parts + i, q * parts + c))
                row_at[q * parts + c] = i * rows - q * out_rows
                col_at[q * parts + c] = points * f + chunk * p - tile * c
        piece = lax.dynamic_index_in_dim(sums, (me % tall * broad + layer % broad + s) % folds, 0, False)
        piece = lax.ppermute(piece, ("ptg", "img"), pairs)
        here = layer * parts + me
        out = lax.dynamic_update_slice(
            out, piece.astype(jnp.float32), (jnp.asarray(row_at)[here], jnp.asarray(col_at)[here])
        )
    return out


def solution(mesh):
    return jax.shard_map(
        shards,
        mesh=mesh,
        in_specs=(P(None, "img"), P("ptg", "img", None), P("ptg", None, "img"), P("ptg")),
        out_specs=P("ptg", "img"),
        check_vma=False,
    )
```

```python
import jax
import jax.numpy as jnp
import numpy as np
from jax import lax
from jax.experimental import pallas as pl
from jax.experimental.pallas import tpu as pltpu
from jax.sharding import PartitionSpec as P


def make_tables(points):
    angle = 2.0 * np.pi / points * np.arange(points)
    cos_of, sin_of = np.cos(angle), -np.sin(angle)
    index = np.arange(points, dtype=np.int64)
    coarse = index[::8, None] * index[None, :] % points
    fine = index[:8, None] * index[None, :] % points
    return [t[p].astype(np.float32) for p in (coarse, fine) for t in (cos_of, sin_of)]


MESH = pl.DeviceIdType.MESH
BLOCK = 256
CUTS = 2


def dot(a, b, dims=((1,), (0,))):
    return lax.dot_general(a, b, (dims, ((), ())), preferred_element_type=jnp.float32)


def remote(src, dst, send, recv, device):
    return pltpu.make_async_remote_copy(
        src_ref=src, dst_ref=dst, send_sem=send, recv_sem=recv, device_id=device, device_id_type=MESH
    )


def arrived(ref, sem):
    pltpu.make_async_copy(ref, ref, sem).wait()


def kernel(
    image, beam_hbm, counts_hbm, start, coarse_cos_hbm, coarse_sin_hbm, fine_cos, fine_sin,
    out,
    column, coarse_cos, coarse_sin, beam, counts, strip, beamed, row_out, col_in, weighted, back_out, back_in,
    real_in, imag_in, given, terms, sums, pieces, starts, values, weight, sent, recv, mirror, first_out, first_in,
    load_sem, own_sem, image_send, image_recv, row_send, row_recv, back_send, back_recv,
    layer_send, layer_recv, start_send, start_recv, piece_send, piece_recv, count_sem,
):
    parts, rows, tile = strip.shape
    layers, _, chunk = terms.shape
    folds = sums.shape[0]
    points = rows * parts
    wide = counts.shape[1]
    half = wide // 2
    me, layer = lax.axis_index("img"), lax.axis_index("ptg")

    def peer(k):
        return lax.rem(me + k, parts)

    def above(k):
        return lax.rem(layer + k, layers)

    def rows_of(d):
        return pl.ds(pl.multiple_of(d * rows, rows), rows)

    loads = [
        pltpu.make_async_copy(src, dst, load_sem.at[at])
        for at, (src, dst) in enumerate(
            [(counts_hbm, counts), (coarse_cos_hbm, coarse_cos), (coarse_sin_hbm, coarse_sin), (beam_hbm, beam)]
        )
    ]
    mine = pltpu.make_async_copy(image.at[rows_of(me), :], strip.at[me], own_sem)
    mine.start()
    for load in loads:
        load.start()

    barrier = pltpu.get_barrier_semaphore()
    for k in range(1, parts):
        pl.semaphore_signal(barrier, inc=1, device_id=(layer, peer(k)), device_id_type=MESH)
    for k in range(1, layers):
        pl.semaphore_signal(barrier, inc=1, device_id=(above(k), me), device_id_type=MESH)
    tall, broad, per_fold = out.shape[0] // rows, tile // chunk, points // tile
    for a in range(tall):
        for b in range(broad):
            source = (lax.rem(me, per_fold) * broad + b, layer * tall + a)

            @pl.when(jnp.logical_or(source[0] != layer, source[1] != me))
            def _():
                pl.semaphore_signal(barrier, inc=1, device_id=source, device_id_type=MESH)

    def owner(f):
        return lax.div(me, tall), f * per_fold + lax.div(layer, broad)

    def is_mine(f):
        q, c = owner(f)
        return jnp.logical_and(q == layer, c == me)

    local = sum(jnp.where(is_mine(f), 1, 0) for f in range(folds))
    pl.semaphore_wait(barrier, parts + layers - 2 + folds - local)

    def image_copy(k):
        d = peer(k)
        return remote(image.at[rows_of(d), :], strip.at[me], image_send.at[k], image_recv.at[me], (layer, d))

    def start_copy(k):
        return remote(start, starts.at[layer], start_send.at[k], start_recv.at[layer], (above(k), me))

    for k in range(1, parts):
        image_copy(k).start()
    for k in range(1, layers):
        start_copy(k).start()
    starts[layer] = start[...]

    low = me < parts // 2

    def grid(shape):
        return lax.broadcasted_iota(jnp.int32, shape, 0), lax.broadcasted_iota(jnp.int32, shape, 1)

    def ones(where):
        return jnp.where(where, 1.0, 0.0).astype(jnp.bfloat16)

    def at_low(where):
        return jnp.logical_and(where, low)

    def at_high(where):
        return jnp.logical_and(where, jnp.logical_not(low))

    def at_first(where):
        return jnp.logical_and(where, me == 0)

    loads[0].wait()
    values[...] = counts[...].astype(jnp.float32).astype(jnp.bfloat16)
    i, j = grid((wide, sent.shape[1]))
    sel = at_low((i == half + j) & (j < half)) | at_high((i == wide - j) & (j >= 1) & (j < half))
    sent[...] = dot(values[...], ones(sel)).astype(jnp.bfloat16)
    i, j = grid((16, wide))
    first_out[...] = dot(ones(i + j == 0), values[...], ((1,), (1,))).astype(jnp.bfloat16)
    other = lax.rem(parts - me, parts)
    other = jnp.where(me == 0, parts // 2, jnp.where(me == parts // 2, 0, other))
    count_copy = remote(sent, recv, count_sem.at[0], count_sem.at[1], (layer, parts - 1 - me))
    first_copy = remote(first_out, first_in, count_sem.at[2], count_sem.at[3], (layer, other))
    count_copy.start()
    first_copy.start()

    loads[1].wait()
    loads[2].wait()

    @pl.loop(0, points // 64)
    def _(g):
        eight = pl.ds(pl.multiple_of(g * 8, 8), 8)
        for c in range(0, points, 256):
            at = pl.ds(c, 256)
            cos_a, sin_a = coarse_cos[eight, at], coarse_sin[eight, at]
            cos_b, sin_b = fine_cos[:, at], fine_sin[:, at]
            for r in range(0, 8, 2):
                cos_rows, sin_rows = [], []
                for t in (r, r + 1):
                    cos_t, sin_t = cos_a[t : t + 1], sin_a[t : t + 1]
                    cos_rows.append(cos_t * cos_b - sin_t * sin_b)
                    sin_rows.append(sin_t * cos_b + cos_t * sin_b)
                to = pl.multiple_of(g * 64 + r * 8, 16)
                column[pl.ds(to, 16), at] = jnp.concatenate(cos_rows, 0).astype(jnp.bfloat16)
                column[pl.ds(points + to, 16), at] = jnp.concatenate(sin_rows, 0).astype(jnp.bfloat16)

    loads[3].wait()

    @pl.loop(0, rows // 8)
    def _(g):
        eight = pl.ds(pl.multiple_of(g * 8, 8), 8)
        turned = beam[eight, :]
        shift = jnp.broadcast_to(start[0:1, 0:1], (8, points))
        step = 1
        while step < points:
            turned = jnp.where((shift & step) != 0, pltpu.roll(turned, step, 1), turned)
            step *= 2
        beam[eight, :] = turned

    mine.wait()
    origin = start[0:1, 0:1]
    for t in range(per_fold):
        for f in range(folds):
            src = t + per_fold * f

            @pl.when(src != me)
            def _():
                arrived(strip.at[src], image_recv.at[src])

        place = lax.broadcasted_iota(jnp.int32, (rows, tile), 1) + t * tile
        window = strip[t + per_fold * (folds - 1)].astype(jnp.float32)
        for f in range(folds - 2, -1, -1):
            window = jnp.where(place + f * points >= origin, strip[t + per_fold * f].astype(jnp.float32), window)
        at = pl.ds(t * tile, tile)
        beamed[:, at] = (beam[:, at] * window).astype(jnp.bfloat16)

    def columns_of(d):
        return pl.ds(pl.multiple_of(d * wide, wide), wide)

    def row_copy(d):
        return remote(row_out.at[d], col_in.at[rows_of(me), :], row_send.at[d], row_recv.at[me], (layer, d))

    _, j = grid((rows, points))
    sides = jnp.where(lax.rem(j, 2) == 0, beamed[...].astype(jnp.float32), -beamed[...].astype(jnp.float32))
    alternating = jnp.sum(sides, 1, keepdims=True)
    _, lane = grid((rows, wide))

    @pl.loop(0, parts // 2)
    def _(step):
        d = lax.rem(me + 1 + step, parts // 2)
        real = dot(beamed[...], column[:points, columns_of(d)])
        imag = dot(beamed[...], column[points:, columns_of(d)])
        imag = jnp.where(jnp.logical_and(lane == 0, d == 0), alternating, imag)
        lower = jnp.where(lane < half, real, pltpu.roll(imag, half, 1)).astype(jnp.bfloat16)
        upper = jnp.where(lane < half, pltpu.roll(real, half, 1), imag).astype(jnp.bfloat16)
        for to, block in ((d, lower), (parts - 1 - d, upper)):

            @pl.when(to == me)
            def _():
                col_in[rows_of(me), :] = block

            @pl.when(to != me)
            def _():
                row_out[to] = block
                row_copy(to).start()

    count_copy.wait()
    first_copy.wait()
    steps = points // BLOCK

    def block_of(b):
        return pl.ds(pl.multiple_of(b * BLOCK, BLOCK), BLOCK)

    i, j = grid((wide, wide))
    own = jnp.logical_and(
        at_low(i == lax.rem(j, half)) | at_high(i == half - lax.rem(j, half)),
        jnp.logical_not(at_first(j == half)),
    )
    own_a, own_b = ones(at_low(own)), ones(at_high(own) | at_first(i + j == 0))
    i, j = grid((recv.shape[1], wide))
    expand = i == lax.rem(j, half)
    recv_a, recv_b = ones(at_high(expand)), ones(at_low(expand))
    i, j = grid((16, wide))
    packed = at_first((i == 0) & (j == half))
    first_a, first_b = ones(packed), ones(packed | at_low((i == 0) & (lax.rem(j, half) == 0) & (me != 0)))
    i, j = grid((BLOCK, BLOCK))
    flip, flip_first = ones(i + j == BLOCK), ones(i + j == 0)
    _, j = grid((1, wide))
    packed = at_first(lax.rem(j, half) == 0)
    scale_row = jnp.where(packed, 0.5, 1.0) * (1.0 / float(points * points))
    sign = jnp.where(packed, 0.0, jnp.where(j < half, -1.0, 1.0))

    mirror[...] = dot(first_in[...], first_b, ((0,), (0,))).astype(jnp.bfloat16)
    weight[...] = dot(first_in[...], first_a, ((0,), (0,))).astype(jnp.bfloat16)

    @pl.loop(0, steps)
    def _(b):
        at = block_of(b)
        total = dot(recv[at, :], recv_b) + dot(values[at, :], own_b)
        mirror[at, :] = (mirror[at, :].astype(jnp.float32) + total).astype(jnp.bfloat16)

    @pl.loop(0, steps)
    def _(b):
        at = block_of(b)
        total = dot(flip, mirror[block_of(steps - 1 - b), :])
        total += dot(flip_first, mirror[block_of(lax.rem(steps - b, steps)), :])
        total += dot(values[at, :], own_a) + dot(recv[at, :], recv_a)
        weight[at, :] = ((weight[at, :].astype(jnp.float32) + total) * scale_row).astype(jnp.bfloat16)

    for k in range(1, parts):
        src = lax.rem(me + parts - k, parts)
        arrived(col_in.at[rows_of(src), :], row_recv.at[src])

    @pl.loop(0, steps)
    def _(b):
        at = block_of(b)
        low = block_of(b + steps)
        cos_part = dot(column[at, :], col_in[...])
        sin_part = dot(column[low, :], col_in[...])
        scale = weight[at, :].astype(jnp.float32)
        weighted[at, :] = (scale * (cos_part + sign * pltpu.roll(sin_part, half, 1))).astype(jnp.bfloat16)
        weighted[low, :] = (scale * (sin_part - sign * pltpu.roll(cos_part, half, 1))).astype(jnp.bfloat16)

    cut = rows // CUTS

    def cut_of(h):
        return pl.ds(h * cut, cut)

    def inverse(d, h):
        at = pl.ds(pl.multiple_of(d * rows + h * cut, cut), cut)
        low = pl.ds(pl.multiple_of((d + parts) * rows + h * cut, cut), cut)
        upper = dot(column[at, :], weighted[:points, :])
        return (upper + dot(column[low, :], weighted[points:, :])).astype(jnp.bfloat16)

    def back_copy(k, h):
        d = peer(k)
        return remote(
            back_out.at[d, cut_of(h), :], back_in.at[me, cut_of(h), :],
            back_send.at[h * parts + k], back_recv.at[h * parts + me], (layer, d),
        )

    for h in range(CUTS):

        @pl.loop(1, parts)
        def _(k):
            d = peer(k)
            back_out[d, cut_of(h), :] = inverse(d, h)
            back_copy(k, h).start()

        back_in[me, cut_of(h), :] = inverse(me, h)

    def chunk_of(q):
        return pl.ds(pl.multiple_of(q * chunk, chunk), chunk)

    def contribution(q, h):
        pixels = dot(real_in[cut_of(h), :], column[: points // 2, chunk_of(q)])
        pixels += dot(imag_in[cut_of(h), :], column[points : points + points // 2, chunk_of(q)])
        middle = imag_in[cut_of(h), 0:1].astype(jnp.float32)
        _, at = grid((cut, chunk))
        pixels += jnp.where(lax.rem(at, 2) == 0, middle, -middle)
        return (beam[cut_of(h), chunk_of(q)] * pixels).astype(jnp.bfloat16)

    def layer_copy(k, h):
        q = above(k)
        return remote(
            given.at[q, cut_of(h), :], terms.at[layer, cut_of(h), :],
            layer_send.at[h * layers + k], layer_recv.at[h * layers + layer], (q, me),
        )

    _, lane = grid((cut, wide))
    for h in range(CUTS):
        for k in range(1, parts):
            src = lax.rem(me + parts - k, parts)
            arrived(back_in.at[src, cut_of(h), :], back_recv.at[h * parts + src])
        for d in range(parts // 2):
            lower = back_in[d, cut_of(h), :].astype(jnp.float32)
            upper = back_in[parts - 1 - d, cut_of(h), :].astype(jnp.float32)
            at = pl.ds(d * wide, wide)
            real_in[cut_of(h), at] = jnp.where(lane < half, lower, pltpu.roll(upper, half, 1)).astype(jnp.bfloat16)
            imag_in[cut_of(h), at] = jnp.where(lane < half, pltpu.roll(lower, half, 1), upper).astype(jnp.bfloat16)

        @pl.loop(1, layers)
        def _(k):
            q = above(k)
            given[q, cut_of(h), :] = contribution(q, h)
            layer_copy(k, h).start()

        terms[layer, cut_of(h), :] = contribution(layer, h)

    slot = lax.rem(me, tall) * broad + lax.rem(layer, broad)
    slots = tall * broad

    def piece_copy(f, h):
        return remote(
            sums.at[f, cut_of(h), :], pieces.at[slot, cut_of(h), :],
            piece_send.at[h * folds + f], piece_recv.at[h * slots + slot], owner(f),
        )

    place = lax.broadcasted_iota(jnp.int32, (cut, chunk), 1) + layer * chunk
    for h in range(CUTS):
        for k in range(1, layers):
            src = lax.rem(layer + layers - k, layers)
            if h == 0:
                arrived(starts.at[src], start_recv.at[src])
            arrived(terms.at[src, cut_of(h), :], layer_recv.at[h * layers + src])
        for f in range(folds):
            total = jnp.zeros((cut, chunk), jnp.float32)
            for p in range(layers):
                offset = place + f * points - starts[p][0:1, 0:1]
                inside = (offset >= 0) & (offset < points)
                total += jnp.where(inside, terms[p, cut_of(h), :].astype(jnp.float32), 0.0)
            sums[f, cut_of(h), :] = total.astype(jnp.bfloat16)

            @pl.when(is_mine(f))
            def _():
                pieces[slot, cut_of(h), :] = sums[f, cut_of(h), :]

            @pl.when(jnp.logical_not(is_mine(f)))
            def _():
                piece_copy(f, h).start()

    for h in range(CUTS):
        for a in range(tall):
            for b in range(broad):
                q, c = lax.rem(me, per_fold) * broad + b, layer * tall + a

                @pl.when(jnp.logical_or(q != layer, c != me))
                def _():
                    at = a * broad + b
                    arrived(pieces.at[at, cut_of(h), :], piece_recv.at[h * slots + at])

                to = pl.ds(a * rows + h * cut, cut)
                out[to, pl.ds(b * chunk, chunk)] = pieces[a * broad + b, cut_of(h), :].astype(jnp.float32)

    for k in range(1, parts):
        image_copy(k).wait_send()
        for h in range(CUTS):
            back_copy(k, h).wait_send()
        row_copy(peer(k)).wait_send()
    for k in range(1, layers):
        start_copy(k).wait_send()
        for h in range(CUTS):
            layer_copy(k, h).wait_send()
    for f in range(folds):

        @pl.when(jnp.logical_not(is_mine(f)))
        def _():
            for h in range(CUTS):
                piece_copy(f, h).wait_send()


def strips(image, beam, counts, start, layers):
    points, wide = counts.shape
    rows, tile = beam.shape[0], image.shape[1]
    parts = points // rows
    folds = tile * parts // points
    chunk = points // layers
    coarse_cos, coarse_sin, fine_cos, fine_sin = (jnp.asarray(t) for t in make_tables(points))
    hp = max(wide // 2, 128)
    slots = points // layers // rows * (tile // chunk)
    vmem, hbm = pl.BlockSpec(memory_space=pltpu.VMEM), pl.BlockSpec(memory_space=pl.ANY)
    bf = jnp.bfloat16
    dma = pltpu.SemaphoreType.DMA
    return pl.pallas_call(
        kernel,
        out_shape=jax.ShapeDtypeStruct((points // layers, tile), jnp.float32),
        in_specs=[hbm, hbm, hbm, vmem, hbm, hbm, vmem, vmem],
        out_specs=vmem,
        scratch_shapes=[
            pltpu.VMEM((2 * points, points), bf),
            pltpu.VMEM((points // 8, points), jnp.float32),
            pltpu.VMEM((points // 8, points), jnp.float32),
            pltpu.VMEM((rows, points), jnp.float32),
            pltpu.VMEM((points, wide), jnp.int32),
            pltpu.VMEM((parts, rows, tile), bf),
            pltpu.VMEM((rows, points), bf),
            pltpu.VMEM((parts, rows, wide), bf),
            pltpu.VMEM((points, wide), bf),
            pltpu.VMEM((2 * points, wide), bf),
            pltpu.VMEM((parts, rows, wide), bf),
            pltpu.VMEM((parts, rows, wide), bf),
            pltpu.VMEM((rows, points // 2), bf),
            pltpu.VMEM((rows, points // 2), bf),
            pltpu.VMEM((layers, rows, chunk), bf),
            pltpu.VMEM((layers, rows, chunk), bf),
            pltpu.VMEM((folds, rows, chunk), bf),
            pltpu.VMEM((slots, rows, chunk), bf),
            pltpu.VMEM((layers, 8, 128), jnp.int32),
            pltpu.VMEM((points, wide), bf),
            pltpu.VMEM((points, wide), bf),
            pltpu.VMEM((points, hp), bf),
            pltpu.VMEM((points, hp), bf),
            pltpu.VMEM((points, wide), bf),
            pltpu.VMEM((16, points), bf),
            pltpu.VMEM((16, points), bf),
            dma((4,)), dma(()), dma((parts,)), dma((parts,)), dma((parts,)), dma((parts,)),
            dma((CUTS * parts,)), dma((CUTS * parts,)), dma((CUTS * layers,)), dma((CUTS * layers,)),
            dma((layers,)), dma((layers,)), dma((CUTS * folds,)), dma((CUTS * slots,)), dma((4,)),
        ],
        compiler_params=pltpu.CompilerParams(
            collective_id=0, has_side_effects=True, vmem_limit_bytes=60 * 1024 * 1024
        ),
    )(image, beam, counts, start, coarse_cos, coarse_sin, fine_cos, fine_sin)


def shards(image, beam, counts, offsets):
    start = jnp.full((8, 128), offsets[0], jnp.int32)
    return strips(image, beam[0], counts[0], start, lax.axis_size("ptg"))


def solution(mesh):
    return jax.shard_map(
        shards,
        mesh=mesh,
        in_specs=(P(None, "img"), P("ptg", "img", None), P("ptg", None, "img"), P("ptg")),
        out_specs=P("ptg", "img"),
        check_vma=False,
    )
```

```python
import jax
import jax.numpy as jnp
import numpy as np
from jax import lax
from jax.experimental import pallas as pl
from jax.experimental.pallas import tpu as pltpu
from jax.sharding import PartitionSpec as P


def make_tables(points):
    angle = 2.0 * np.pi / points * np.arange(points)
    cos_of, sin_of = np.cos(angle), -np.sin(angle)
    index = np.arange(points, dtype=np.int64)
    coarse = index[::8, None] * index[None, :] % points
    fine = index[:8, None] * index[None, :] % points
    return [t[p].astype(np.float32) for p in (coarse, fine) for t in (cos_of, sin_of)]


MESH = pl.DeviceIdType.MESH
BLOCK = 256
CUTS = 2


def dot(a, b, dims=((1,), (0,))):
    return lax.dot_general(a, b, (dims, ((), ())), preferred_element_type=jnp.float32)


def remote(src, dst, send, recv, device):
    return pltpu.make_async_remote_copy(
        src_ref=src, dst_ref=dst, send_sem=send, recv_sem=recv, device_id=device, device_id_type=MESH
    )


def arrived(ref, sem):
    pltpu.make_async_copy(ref, ref, sem).wait()


def kernel(
    image, beam_hbm, counts_hbm, start, coarse_cos_hbm, coarse_sin_hbm, fine_cos, fine_sin,
    out,
    column, coarse_cos, coarse_sin, beam, counts, strip, beamed, row_out, col_in, weighted, back_out, back_in,
    real_in, imag_in, given, terms, sums, pieces, starts, values, weight, sent, recv, mirror, first_out, first_in,
    load_sem, own_sem, image_send, image_recv, row_send, row_recv, back_send, back_recv,
    layer_send, layer_recv, start_send, start_recv, piece_send, piece_recv, count_sem,
):
    parts, rows, tile = strip.shape
    layers, _, chunk = terms.shape
    folds = sums.shape[0]
    points = rows * parts
    wide = counts.shape[1]
    half = wide // 2
    me, layer = lax.axis_index("img"), lax.axis_index("ptg")

    def peer(k):
        return lax.rem(me + k, parts)

    def above(k):
        return lax.rem(layer + k, layers)

    def rows_of(d):
        return pl.ds(pl.multiple_of(d * rows, rows), rows)

    loads = [
        pltpu.make_async_copy(src, dst, load_sem.at[at])
        for at, (src, dst) in enumerate(
            [(counts_hbm, counts), (coarse_cos_hbm, coarse_cos), (coarse_sin_hbm, coarse_sin), (beam_hbm, beam)]
        )
    ]
    mine = pltpu.make_async_copy(image.at[rows_of(me), :], strip.at[me], own_sem)
    mine.start()
    for load in loads:
        load.start()

    barrier = pltpu.get_barrier_semaphore()
    for k in range(1, parts):
        pl.semaphore_signal(barrier, inc=1, device_id=(layer, peer(k)), device_id_type=MESH)
    for k in range(1, layers):
        pl.semaphore_signal(barrier, inc=1, device_id=(above(k), me), device_id_type=MESH)
    tall, broad, per_fold = out.shape[0] // rows, tile // chunk, points // tile
    for a in range(tall):
        for b in range(broad):
            source = (lax.rem(me, per_fold) * broad + b, layer * tall + a)

            @pl.when(jnp.logical_or(source[0] != layer, source[1] != me))
            def _():
                pl.semaphore_signal(barrier, inc=1, device_id=source, device_id_type=MESH)

    def owner(f):
        return lax.div(me, tall), f * per_fold + lax.div(layer, broad)

    def is_mine(f):
        q, c = owner(f)
        return jnp.logical_and(q == layer, c == me)

    local = sum(jnp.where(is_mine(f), 1, 0) for f in range(folds))
    pl.semaphore_wait(barrier, parts + layers - 2 + folds - local)

    cut = rows // CUTS

    def cut_of(h):
        return pl.ds(h * cut, cut)

    def image_copy(k, h):
        d = peer(k)
        return remote(
            image.at[pl.ds(pl.multiple_of(d * rows + h * cut, cut), cut), :], strip.at[me, cut_of(h), :],
            image_send.at[h * parts + k], image_recv.at[h * parts + me], (layer, d),
        )

    def start_copy(k):
        return remote(start, starts.at[layer], start_send.at[k], start_recv.at[layer], (above(k), me))

    for h in range(CUTS):
        for k in range(1, parts):
            image_copy(k, h).start()
    for k in range(1, layers):
        start_copy(k).start()
    starts[layer] = start[...]

    low = me < parts // 2

    def grid(shape):
        return lax.broadcasted_iota(jnp.int32, shape, 0), lax.broadcasted_iota(jnp.int32, shape, 1)

    def ones(where):
        return jnp.where(where, 1.0, 0.0).astype(jnp.bfloat16)

    def at_low(where):
        return jnp.logical_and(where, low)

    def at_high(where):
        return jnp.logical_and(where, jnp.logical_not(low))

    def at_first(where):
        return jnp.logical_and(where, me == 0)

    loads[0].wait()
    values[...] = counts[...].astype(jnp.float32).astype(jnp.bfloat16)
    i, j = grid((wide, sent.shape[1]))
    sel = at_low((i == half + j) & (j < half)) | at_high((i == wide - j) & (j >= 1) & (j < half))
    sent[...] = dot(values[...], ones(sel)).astype(jnp.bfloat16)
    i, j = grid((16, wide))
    first_out[...] = dot(ones(i + j == 0), values[...], ((1,), (1,))).astype(jnp.bfloat16)
    other = lax.rem(parts - me, parts)
    other = jnp.where(me == 0, parts // 2, jnp.where(me == parts // 2, 0, other))
    count_copy = remote(sent, recv, count_sem.at[0], count_sem.at[1], (layer, parts - 1 - me))
    first_copy = remote(first_out, first_in, count_sem.at[2], count_sem.at[3], (layer, other))
    count_copy.start()
    first_copy.start()

    loads[1].wait()
    loads[2].wait()

    @pl.loop(0, points // 64)
    def _(g):
        eight = pl.ds(pl.multiple_of(g * 8, 8), 8)
        for c in range(0, points, 256):
            at = pl.ds(c, 256)
            cos_a, sin_a = coarse_cos[eight, at], coarse_sin[eight, at]
            cos_b, sin_b = fine_cos[:, at], fine_sin[:, at]
            for r in range(0, 8, 2):
                cos_rows, sin_rows = [], []
                for t in (r, r + 1):
                    cos_t, sin_t = cos_a[t : t + 1], sin_a[t : t + 1]
                    cos_rows.append(cos_t * cos_b - sin_t * sin_b)
                    sin_rows.append(sin_t * cos_b + cos_t * sin_b)
                to = pl.multiple_of(g * 64 + r * 8, 16)
                column[pl.ds(to, 16), at] = jnp.concatenate(cos_rows, 0).astype(jnp.bfloat16)
                column[pl.ds(points + to, 16), at] = jnp.concatenate(sin_rows, 0).astype(jnp.bfloat16)

    loads[3].wait()

    @pl.loop(0, rows // 8, unroll=4)
    def _(g):
        eight = pl.ds(pl.multiple_of(g * 8, 8), 8)
        turned = beam[eight, :]
        shift = jnp.broadcast_to(start[0:1, 0:1], (8, points))
        step = 1
        while step < points:
            turned = jnp.where((shift & step) != 0, pltpu.roll(turned, step, 1), turned)
            step *= 2
        beam[eight, :] = turned

    mine.wait()
    origin = start[0:1, 0:1]
    def window_cut(h):
        for t in range(per_fold):
            for f in range(folds):
                src = t + per_fold * f

                @pl.when(src != me)
                def _():
                    arrived(strip.at[src, cut_of(h), :], image_recv.at[h * parts + src])

            place = lax.broadcasted_iota(jnp.int32, (cut, tile), 1) + t * tile
            window = strip[t + per_fold * (folds - 1), cut_of(h), :].astype(jnp.float32)
            for f in range(folds - 2, -1, -1):
                other = strip[t + per_fold * f, cut_of(h), :].astype(jnp.float32)
                window = jnp.where(place + f * points >= origin, other, window)
            at = pl.ds(t * tile, tile)
            beamed[cut_of(h), at] = (beam[cut_of(h), at] * window).astype(jnp.bfloat16)

    def columns_of(d):
        return pl.ds(pl.multiple_of(d * wide, wide), wide)

    def row_copy(d, h):
        to = pl.ds(pl.multiple_of(me * rows + h * cut, cut), cut)
        return remote(
            row_out.at[d, cut_of(h), :], col_in.at[to, :],
            row_send.at[h * parts + d], row_recv.at[h * parts + me], (layer, d),
        )

    _, column_at = grid((cut, points))
    _, lane = grid((cut, wide))
    for h in range(CUTS):
        window_cut(h)
        pixels = beamed[cut_of(h), :].astype(jnp.float32)
        alternating = jnp.sum(jnp.where(lax.rem(column_at, 2) == 0, pixels, -pixels), 1, keepdims=True)

        @pl.loop(0, parts // 2)
        def _(step):
            d = lax.rem(me + 1 + step, parts // 2)
            real = dot(beamed[cut_of(h), :], column[:points, columns_of(d)])
            imag = dot(beamed[cut_of(h), :], column[points:, columns_of(d)])
            imag = jnp.where(jnp.logical_and(lane == 0, d == 0), alternating, imag)
            lower = jnp.where(lane < half, real, pltpu.roll(imag, half, 1)).astype(jnp.bfloat16)
            upper = jnp.where(lane < half, pltpu.roll(real, half, 1), imag).astype(jnp.bfloat16)
            for to, block in ((d, lower), (parts - 1 - d, upper)):

                @pl.when(to == me)
                def _():
                    col_in[pl.ds(pl.multiple_of(me * rows + h * cut, cut), cut), :] = block

                @pl.when(to != me)
                def _():
                    row_out[to, cut_of(h), :] = block
                    row_copy(to, h).start()

    count_copy.wait()
    first_copy.wait()
    steps = points // BLOCK

    def block_of(b):
        return pl.ds(pl.multiple_of(b * BLOCK, BLOCK), BLOCK)

    i, j = grid((wide, wide))
    own = jnp.logical_and(
        at_low(i == lax.rem(j, half)) | at_high(i == half - lax.rem(j, half)),
        jnp.logical_not(at_first(j == half)),
    )
    own_a, own_b = ones(at_low(own)), ones(at_high(own) | at_first(i + j == 0))
    i, j = grid((recv.shape[1], wide))
    expand = i == lax.rem(j, half)
    recv_a, recv_b = ones(at_high(expand)), ones(at_low(expand))
    i, j = grid((16, wide))
    packed = at_first((i == 0) & (j == half))
    first_a, first_b = ones(packed), ones(packed | at_low((i == 0) & (lax.rem(j, half) == 0) & (me != 0)))
    i, j = grid((BLOCK, BLOCK))
    flip, flip_first = ones(i + j == BLOCK), ones(i + j == 0)
    _, j = grid((1, wide))
    packed = at_first(lax.rem(j, half) == 0)
    scale_row = jnp.where(packed, 0.5, 1.0) * (1.0 / float(points * points))
    sign = jnp.where(packed, 0.0, jnp.where(j < half, -1.0, 1.0))

    mirror[...] = dot(first_in[...], first_b, ((0,), (0,))).astype(jnp.bfloat16)
    weight[...] = dot(first_in[...], first_a, ((0,), (0,))).astype(jnp.bfloat16)

    @pl.loop(0, steps, unroll=4)
    def _(b):
        at = block_of(b)
        total = dot(recv[at, :], recv_b) + dot(values[at, :], own_b)
        mirror[at, :] = (mirror[at, :].astype(jnp.float32) + total).astype(jnp.bfloat16)

    @pl.loop(0, steps, unroll=4)
    def _(b):
        at = block_of(b)
        total = dot(flip, mirror[block_of(steps - 1 - b), :])
        total += dot(flip_first, mirror[block_of(lax.rem(steps - b, steps)), :])
        total += dot(values[at, :], own_a) + dot(recv[at, :], recv_a)
        weight[at, :] = ((weight[at, :].astype(jnp.float32) + total) * scale_row).astype(jnp.bfloat16)

    for k in range(1, parts):
        src = lax.rem(me + parts - k, parts)
        for h in range(CUTS):
            at = pl.ds(pl.multiple_of(src * rows + h * cut, cut), cut)
            arrived(col_in.at[at, :], row_recv.at[h * parts + src])

    @pl.loop(0, steps, unroll=2)
    def _(b):
        at = block_of(b)
        low = block_of(b + steps)
        cos_part = dot(column[at, :], col_in[...])
        sin_part = dot(column[low, :], col_in[...])
        scale = weight[at, :].astype(jnp.float32)
        weighted[at, :] = (scale * (cos_part + sign * pltpu.roll(sin_part, half, 1))).astype(jnp.bfloat16)
        weighted[low, :] = (scale * (sin_part - sign * pltpu.roll(cos_part, half, 1))).astype(jnp.bfloat16)

    def inverse(d, h):
        at = pl.ds(pl.multiple_of(d * rows + h * cut, cut), cut)
        low = pl.ds(pl.multiple_of((d + parts) * rows + h * cut, cut), cut)
        upper = dot(column[at, :], weighted[:points, :])
        return (upper + dot(column[low, :], weighted[points:, :])).astype(jnp.bfloat16)

    def back_copy(k, h):
        d = peer(k)
        return remote(
            back_out.at[d, cut_of(h), :], back_in.at[me, cut_of(h), :],
            back_send.at[h * parts + k], back_recv.at[h * parts + me], (layer, d),
        )

    for h in range(CUTS):

        @pl.loop(1, parts)
        def _(k):
            d = peer(k)
            back_out[d, cut_of(h), :] = inverse(d, h)
            back_copy(k, h).start()

        back_in[me, cut_of(h), :] = inverse(me, h)

    def chunk_of(q):
        return pl.ds(pl.multiple_of(q * chunk, chunk), chunk)

    def contribution(q, h):
        pixels = dot(real_in[cut_of(h), :], column[: points // 2, chunk_of(q)])
        pixels += dot(imag_in[cut_of(h), :], column[points : points + points // 2, chunk_of(q)])
        middle = imag_in[cut_of(h), 0:1].astype(jnp.float32)
        _, at = grid((cut, chunk))
        pixels += jnp.where(lax.rem(at, 2) == 0, middle, -middle)
        return (beam[cut_of(h), chunk_of(q)] * pixels).astype(jnp.bfloat16)

    def layer_copy(k, h):
        q = above(k)
        return remote(
            given.at[q, cut_of(h), :], terms.at[layer, cut_of(h), :],
            layer_send.at[h * layers + k], layer_recv.at[h * layers + layer], (q, me),
        )

    for h in range(CUTS):
        for k in range(1, parts):
            src = lax.rem(me + parts - k, parts)
            arrived(back_in.at[src, cut_of(h), :], back_recv.at[h * parts + src])
        for d in range(parts // 2):
            lower = back_in[d, cut_of(h), :].astype(jnp.float32)
            upper = back_in[parts - 1 - d, cut_of(h), :].astype(jnp.float32)
            at = pl.ds(d * wide, wide)
            real_in[cut_of(h), at] = jnp.where(lane < half, lower, pltpu.roll(upper, half, 1)).astype(jnp.bfloat16)
            imag_in[cut_of(h), at] = jnp.where(lane < half, pltpu.roll(lower, half, 1), upper).astype(jnp.bfloat16)

        @pl.loop(1, layers)
        def _(k):
            q = above(k)
            given[q, cut_of(h), :] = contribution(q, h)
            layer_copy(k, h).start()

        terms[layer, cut_of(h), :] = contribution(layer, h)

    slot = lax.rem(me, tall) * broad + lax.rem(layer, broad)
    slots = tall * broad

    def piece_copy(f, h):
        return remote(
            sums.at[f, cut_of(h), :], pieces.at[slot, cut_of(h), :],
            piece_send.at[h * folds + f], piece_recv.at[h * slots + slot], owner(f),
        )

    place = lax.broadcasted_iota(jnp.int32, (cut, chunk), 1) + layer * chunk
    for h in range(CUTS):
        for k in range(1, layers):
            src = lax.rem(layer + layers - k, layers)
            if h == 0:
                arrived(starts.at[src], start_recv.at[src])
            arrived(terms.at[src, cut_of(h), :], layer_recv.at[h * layers + src])
        for f in range(folds):
            total = jnp.zeros((cut, chunk), jnp.float32)
            for p in range(layers):
                offset = place + f * points - starts[p][0:1, 0:1]
                inside = (offset >= 0) & (offset < points)
                total += jnp.where(inside, terms[p, cut_of(h), :].astype(jnp.float32), 0.0)
            sums[f, cut_of(h), :] = total.astype(jnp.bfloat16)

            @pl.when(is_mine(f))
            def _():
                pieces[slot, cut_of(h), :] = sums[f, cut_of(h), :]

            @pl.when(jnp.logical_not(is_mine(f)))
            def _():
                piece_copy(f, h).start()

    for h in range(CUTS):
        for a in range(tall):
            for b in range(broad):
                q, c = lax.rem(me, per_fold) * broad + b, layer * tall + a

                @pl.when(jnp.logical_or(q != layer, c != me))
                def _():
                    at = a * broad + b
                    arrived(pieces.at[at, cut_of(h), :], piece_recv.at[h * slots + at])

                to = pl.ds(a * rows + h * cut, cut)
                out[to, pl.ds(b * chunk, chunk)] = pieces[a * broad + b, cut_of(h), :]

    for k in range(1, parts):
        for h in range(CUTS):
            image_copy(k, h).wait_send()
            row_copy(peer(k), h).wait_send()
            back_copy(k, h).wait_send()
    for k in range(1, layers):
        start_copy(k).wait_send()
        for h in range(CUTS):
            layer_copy(k, h).wait_send()
    for f in range(folds):

        @pl.when(jnp.logical_not(is_mine(f)))
        def _():
            for h in range(CUTS):
                piece_copy(f, h).wait_send()


def strips(image, beam, counts, start, layers):
    points, wide = counts.shape
    rows, tile = beam.shape[0], image.shape[1]
    parts = points // rows
    folds = tile * parts // points
    chunk = points // layers
    coarse_cos, coarse_sin, fine_cos, fine_sin = (jnp.asarray(t) for t in make_tables(points))
    hp = max(wide // 2, 128)
    slots = points // layers // rows * (tile // chunk)
    vmem, hbm = pl.BlockSpec(memory_space=pltpu.VMEM), pl.BlockSpec(memory_space=pl.ANY)
    bf = jnp.bfloat16
    dma = pltpu.SemaphoreType.DMA
    return pl.pallas_call(
        kernel,
        out_shape=jax.ShapeDtypeStruct((points // layers, tile), bf),
        in_specs=[hbm, hbm, hbm, vmem, hbm, hbm, vmem, vmem],
        out_specs=vmem,
        scratch_shapes=[
            pltpu.VMEM((2 * points, points), bf),
            pltpu.VMEM((points // 8, points), jnp.float32),
            pltpu.VMEM((points // 8, points), jnp.float32),
            pltpu.VMEM((rows, points), jnp.float32),
            pltpu.VMEM((points, wide), jnp.int32),
            pltpu.VMEM((parts, rows, tile), bf),
            pltpu.VMEM((rows, points), bf),
            pltpu.VMEM((parts, rows, wide), bf),
            pltpu.VMEM((points, wide), bf),
            pltpu.VMEM((2 * points, wide), bf),
            pltpu.VMEM((parts, rows, wide), bf),
            pltpu.VMEM((parts, rows, wide), bf),
            pltpu.VMEM((rows, points // 2), bf),
            pltpu.VMEM((rows, points // 2), bf),
            pltpu.VMEM((layers, rows, chunk), bf),
            pltpu.VMEM((layers, rows, chunk), bf),
            pltpu.VMEM((folds, rows, chunk), bf),
            pltpu.VMEM((slots, rows, chunk), bf),
            pltpu.VMEM((layers, 8, 128), jnp.int32),
            pltpu.VMEM((points, wide), bf),
            pltpu.VMEM((points, wide), bf),
            pltpu.VMEM((points, hp), bf),
            pltpu.VMEM((points, hp), bf),
            pltpu.VMEM((points, wide), bf),
            pltpu.VMEM((16, points), bf),
            pltpu.VMEM((16, points), bf),
            dma((4,)), dma(()), dma((CUTS * parts,)), dma((CUTS * parts,)), dma((CUTS * parts,)), dma((CUTS * parts,)),
            dma((CUTS * parts,)), dma((CUTS * parts,)), dma((CUTS * layers,)), dma((CUTS * layers,)),
            dma((layers,)), dma((layers,)), dma((CUTS * folds,)), dma((CUTS * slots,)), dma((4,)),
        ],
        compiler_params=pltpu.CompilerParams(
            collective_id=0, has_side_effects=True, vmem_limit_bytes=60 * 1024 * 1024
        ),
    )(image, beam, counts, start, coarse_cos, coarse_sin, fine_cos, fine_sin)


def shards(image, beam, counts, offsets):
    start = jnp.full((8, 128), offsets[0], jnp.int32)
    return strips(image, beam[0], counts[0], start, lax.axis_size("ptg")).astype(jnp.float32)


def solution(mesh):
    return jax.shard_map(
        shards,
        mesh=mesh,
        in_specs=(P(None, "img"), P("ptg", "img", None), P("ptg", None, "img"), P("ptg")),
        out_specs=P("ptg", "img"),
        check_vma=False,
    )
```

```python
import jax
import jax.numpy as jnp
import numpy as np
from jax import lax
from jax.experimental import pallas as pl
from jax.experimental.pallas import tpu as pltpu
from jax.sharding import PartitionSpec as P


def make_tables(points):
    angle = 2.0 * np.pi / points * np.arange(points)
    cos_of, sin_of = np.cos(angle), -np.sin(angle)
    index = np.arange(points, dtype=np.int64)
    coarse = index[::8, None] * index[None, :] % points
    fine = index[:8, None] * index[None, :] % points
    return [t[p].astype(np.float32) for p in (coarse, fine) for t in (cos_of, sin_of)]


MESH = pl.DeviceIdType.MESH
BLOCK = 256
CUTS = 2


def dot(a, b, dims=((1,), (0,))):
    return lax.dot_general(a, b, (dims, ((), ())), preferred_element_type=jnp.float32)


def remote(src, dst, send, recv, device):
    return pltpu.make_async_remote_copy(
        src_ref=src, dst_ref=dst, send_sem=send, recv_sem=recv, device_id=device, device_id_type=MESH
    )


def arrived(ref, sem):
    pltpu.make_async_copy(ref, ref, sem).wait()


def kernel(
    image, beam_hbm, counts_hbm, start, coarse_cos_hbm, coarse_sin_hbm, fine_cos, fine_sin,
    out,
    column, coarse_cos, coarse_sin, beam, counts, strip, beamed, row_out, col_in, weighted, back_out, back_in,
    real_in, imag_in, given, gathered, terms, sums, pieces, starts, values, weight, sent, recv, mirror, first_out, first_in,
    load_sem, own_sem, image_send, image_recv, row_send, row_recv, back_send, back_recv,
    give_send, give_recv, layer_send, layer_recv, start_send, start_recv, piece_send, piece_recv, count_sem,
):
    parts, rows, tile = strip.shape
    layers, folds, sub = terms.shape[1], sums.shape[1], terms.shape[3]
    points = rows * parts
    wide = counts.shape[1]
    half = wide // 2
    me, layer = lax.axis_index("img"), lax.axis_index("ptg")

    def peer(k):
        return lax.rem(me + k, parts)

    def above(k):
        return lax.rem(layer + k, layers)

    def rows_of(d):
        return pl.ds(pl.multiple_of(d * rows, rows), rows)

    loads = [
        pltpu.make_async_copy(src, dst, load_sem.at[at])
        for at, (src, dst) in enumerate(
            [(counts_hbm, counts), (coarse_cos_hbm, coarse_cos), (coarse_sin_hbm, coarse_sin), (beam_hbm, beam)]
        )
    ]
    mine = pltpu.make_async_copy(image.at[rows_of(me), :], strip.at[me], own_sem)
    mine.start()
    for load in loads:
        load.start()

    barrier = pltpu.get_barrier_semaphore()
    for k in range(1, parts):
        pl.semaphore_signal(barrier, inc=1, device_id=(layer, peer(k)), device_id_type=MESH)
    for k in range(1, layers):
        pl.semaphore_signal(barrier, inc=1, device_id=(above(k), me), device_id_type=MESH)
    pl.semaphore_wait(barrier, parts + layers - 2)
    tall, per_fold = out.shape[0] // rows, points // tile
    cut = rows // CUTS

    def cut_of(h):
        return pl.ds(h * cut, cut)

    def image_copy(k, h):
        d = peer(k)
        return remote(
            image.at[pl.ds(pl.multiple_of(d * rows + h * cut, cut), cut), :], strip.at[me, cut_of(h), :],
            image_send.at[h * parts + k], image_recv.at[h * parts + me], (layer, d),
        )

    def start_copy(k):
        return remote(start, starts.at[layer], start_send.at[k], start_recv.at[layer], (above(k), me))

    for h in range(CUTS):
        for k in range(1, parts):
            image_copy(k, h).start()
    for k in range(1, layers):
        start_copy(k).start()
    starts[layer] = start[...]

    low = me < parts // 2

    def grid(shape):
        return lax.broadcasted_iota(jnp.int32, shape, 0), lax.broadcasted_iota(jnp.int32, shape, 1)

    def ones(where):
        return jnp.where(where, 1.0, 0.0).astype(jnp.bfloat16)

    def at_low(where):
        return jnp.logical_and(where, low)

    def at_high(where):
        return jnp.logical_and(where, jnp.logical_not(low))

    def at_first(where):
        return jnp.logical_and(where, me == 0)

    loads[0].wait()
    values[...] = counts[...].astype(jnp.float32).astype(jnp.bfloat16)
    i, j = grid((wide, sent.shape[1]))
    sel = at_low((i == half + j) & (j < half)) | at_high((i == wide - j) & (j >= 1) & (j < half))
    sent[...] = dot(values[...], ones(sel)).astype(jnp.bfloat16)
    i, j = grid((16, wide))
    first_out[...] = dot(ones(i + j == 0), values[...], ((1,), (1,))).astype(jnp.bfloat16)
    other = lax.rem(parts - me, parts)
    other = jnp.where(me == 0, parts // 2, jnp.where(me == parts // 2, 0, other))
    count_copy = remote(sent, recv, count_sem.at[0], count_sem.at[1], (layer, parts - 1 - me))
    first_copy = remote(first_out, first_in, count_sem.at[2], count_sem.at[3], (layer, other))
    count_copy.start()
    first_copy.start()

    loads[1].wait()
    loads[2].wait()

    @pl.loop(0, points // 64)
    def _(g):
        eight = pl.ds(pl.multiple_of(g * 8, 8), 8)
        for c in range(0, points, 256):
            at = pl.ds(c, 256)
            cos_a, sin_a = coarse_cos[eight, at], coarse_sin[eight, at]
            cos_b, sin_b = fine_cos[:, at], fine_sin[:, at]
            for r in range(0, 8, 2):
                cos_rows, sin_rows = [], []
                for t in (r, r + 1):
                    cos_t, sin_t = cos_a[t : t + 1], sin_a[t : t + 1]
                    cos_rows.append(cos_t * cos_b - sin_t * sin_b)
                    sin_rows.append(sin_t * cos_b + cos_t * sin_b)
                to = pl.multiple_of(g * 64 + r * 8, 16)
                column[pl.ds(to, 16), at] = jnp.concatenate(cos_rows, 0).astype(jnp.bfloat16)
                column[pl.ds(points + to, 16), at] = jnp.concatenate(sin_rows, 0).astype(jnp.bfloat16)

    loads[3].wait()

    @pl.loop(0, rows // 8, unroll=4)
    def _(g):
        eight = pl.ds(pl.multiple_of(g * 8, 8), 8)
        turned = beam[eight, :]
        shift = jnp.broadcast_to(start[0:1, 0:1], (8, points))
        step = 1
        while step < points:
            turned = jnp.where((shift & step) != 0, pltpu.roll(turned, step, 1), turned)
            step *= 2
        beam[eight, :] = turned

    mine.wait()
    origin = start[0:1, 0:1]
    def window_cut(h):
        for t in range(per_fold):
            for f in range(folds):
                src = t + per_fold * f

                @pl.when(src != me)
                def _():
                    arrived(strip.at[src, cut_of(h), :], image_recv.at[h * parts + src])

            place = lax.broadcasted_iota(jnp.int32, (cut, tile), 1) + t * tile
            window = strip[t + per_fold * (folds - 1), cut_of(h), :].astype(jnp.float32)
            for f in range(folds - 2, -1, -1):
                other = strip[t + per_fold * f, cut_of(h), :].astype(jnp.float32)
                window = jnp.where(place + f * points >= origin, other, window)
            at = pl.ds(t * tile, tile)
            beamed[cut_of(h), at] = (beam[cut_of(h), at] * window).astype(jnp.bfloat16)

    def columns_of(d):
        return pl.ds(pl.multiple_of(d * wide, wide), wide)

    def row_copy(d, h):
        to = pl.ds(pl.multiple_of(me * rows + h * cut, cut), cut)
        return remote(
            row_out.at[d, cut_of(h), :], col_in.at[to, :],
            row_send.at[h * parts + d], row_recv.at[h * parts + me], (layer, d),
        )

    _, column_at = grid((cut, points))
    _, lane = grid((cut, wide))
    for h in range(CUTS):
        window_cut(h)
        pixels = beamed[cut_of(h), :].astype(jnp.float32)
        alternating = jnp.sum(jnp.where(lax.rem(column_at, 2) == 0, pixels, -pixels), 1, keepdims=True)

        @pl.loop(0, parts // 2)
        def _(step):
            d = lax.rem(me + 1 + step, parts // 2)
            real = dot(beamed[cut_of(h), :], column[:points, columns_of(d)])
            imag = dot(beamed[cut_of(h), :], column[points:, columns_of(d)])
            imag = jnp.where(jnp.logical_and(lane == 0, d == 0), alternating, imag)
            lower = jnp.where(lane < half, real, pltpu.roll(imag, half, 1)).astype(jnp.bfloat16)
            upper = jnp.where(lane < half, pltpu.roll(real, half, 1), imag).astype(jnp.bfloat16)
            for to, block in ((d, lower), (parts - 1 - d, upper)):

                @pl.when(to == me)
                def _():
                    col_in[pl.ds(pl.multiple_of(me * rows + h * cut, cut), cut), :] = block

                @pl.when(to != me)
                def _():
                    row_out[to, cut_of(h), :] = block
                    row_copy(to, h).start()

    count_copy.wait()
    first_copy.wait()
    steps = points // BLOCK

    def block_of(b):
        return pl.ds(pl.multiple_of(b * BLOCK, BLOCK), BLOCK)

    i, j = grid((wide, wide))
    own = jnp.logical_and(
        at_low(i == lax.rem(j, half)) | at_high(i == half - lax.rem(j, half)),
        jnp.logical_not(at_first(j == half)),
    )
    own_a, own_b = ones(at_low(own)), ones(at_high(own) | at_first(i + j == 0))
    i, j = grid((recv.shape[1], wide))
    expand = i == lax.rem(j, half)
    recv_a, recv_b = ones(at_high(expand)), ones(at_low(expand))
    i, j = grid((16, wide))
    packed = at_first((i == 0) & (j == half))
    first_a, first_b = ones(packed), ones(packed | at_low((i == 0) & (lax.rem(j, half) == 0) & (me != 0)))
    i, j = grid((BLOCK, BLOCK))
    flip, flip_first = ones(i + j == BLOCK), ones(i + j == 0)
    _, j = grid((1, wide))
    packed = at_first(lax.rem(j, half) == 0)
    scale_row = jnp.where(packed, 0.5, 1.0) * (1.0 / float(points * points))
    sign = jnp.where(packed, 0.0, jnp.where(j < half, -1.0, 1.0))

    mirror[...] = dot(first_in[...], first_b, ((0,), (0,))).astype(jnp.bfloat16)
    weight[...] = dot(first_in[...], first_a, ((0,), (0,))).astype(jnp.bfloat16)

    @pl.loop(0, steps, unroll=4)
    def _(b):
        at = block_of(b)
        total = dot(recv[at, :], recv_b) + dot(values[at, :], own_b)
        mirror[at, :] = (mirror[at, :].astype(jnp.float32) + total).astype(jnp.bfloat16)

    @pl.loop(0, steps, unroll=4)
    def _(b):
        at = block_of(b)
        total = dot(flip, mirror[block_of(steps - 1 - b), :])
        total += dot(flip_first, mirror[block_of(lax.rem(steps - b, steps)), :])
        total += dot(values[at, :], own_a) + dot(recv[at, :], recv_a)
        weight[at, :] = ((weight[at, :].astype(jnp.float32) + total) * scale_row).astype(jnp.bfloat16)

    for k in range(1, parts):
        src = lax.rem(me + parts - k, parts)
        for h in range(CUTS):
            at = pl.ds(pl.multiple_of(src * rows + h * cut, cut), cut)
            arrived(col_in.at[at, :], row_recv.at[h * parts + src])

    @pl.loop(0, steps, unroll=2)
    def _(b):
        at = block_of(b)
        low = block_of(b + steps)
        cos_part = dot(column[at, :], col_in[...])
        sin_part = dot(column[low, :], col_in[...])
        scale = weight[at, :].astype(jnp.float32)
        weighted[at, :] = (scale * (cos_part + sign * pltpu.roll(sin_part, half, 1))).astype(jnp.bfloat16)
        weighted[low, :] = (scale * (sin_part - sign * pltpu.roll(cos_part, half, 1))).astype(jnp.bfloat16)

    def inverse(d, h):
        at = pl.ds(pl.multiple_of(d * rows + h * cut, cut), cut)
        low = pl.ds(pl.multiple_of((d + parts) * rows + h * cut, cut), cut)
        upper = dot(column[at, :], weighted[:points, :])
        return (upper + dot(column[low, :], weighted[points:, :])).astype(jnp.bfloat16)

    def back_copy(k, h):
        d = peer(k)
        return remote(
            back_out.at[d, cut_of(h), :], back_in.at[me, cut_of(h), :],
            back_send.at[h * parts + k], back_recv.at[h * parts + me], (layer, d),
        )

    for h in range(CUTS):

        @pl.loop(1, parts)
        def _(k):
            d = peer(k)
            back_out[d, cut_of(h), :] = inverse(d, h)
            back_copy(k, h).start()

        back_in[me, cut_of(h), :] = inverse(me, h)

    def contribution(t, h):
        at = pl.ds(pl.multiple_of(t * tile, tile), tile)
        pixels = dot(real_in[cut_of(h), :], column[: points // 2, at])
        pixels += dot(imag_in[cut_of(h), :], column[points : points + points // 2, at])
        middle = imag_in[cut_of(h), 0:1].astype(jnp.float32)
        _, place = grid((cut, tile))
        pixels += jnp.where(lax.rem(place, 2) == 0, middle, -middle)
        return (beam[cut_of(h), at] * pixels).astype(jnp.bfloat16)

    def give_copy(c, h):
        return remote(
            given.at[h, c], gathered.at[h, me],
            give_send.at[h * parts + c], give_recv.at[h * parts + me], (layer, c),
        )

    for h in range(CUTS):
        for k in range(1, parts):
            src = lax.rem(me + parts - k, parts)
            arrived(back_in.at[src, cut_of(h), :], back_recv.at[h * parts + src])
        for d in range(parts // 2):
            lower = back_in[d, cut_of(h), :].astype(jnp.float32)
            upper = back_in[parts - 1 - d, cut_of(h), :].astype(jnp.float32)
            at = pl.ds(d * wide, wide)
            real_in[cut_of(h), at] = jnp.where(lane < half, lower, pltpu.roll(upper, half, 1)).astype(jnp.bfloat16)
            imag_in[cut_of(h), at] = jnp.where(lane < half, pltpu.roll(lower, half, 1), upper).astype(jnp.bfloat16)

        @pl.loop(0, per_fold)
        def _(step):
            t = lax.rem(me + 1 + step, per_fold)
            block = contribution(t, h)
            for f in range(folds):
                c = t + per_fold * f
                share = block[f * sub : (f + 1) * sub]

                @pl.when(c == me)
                def _():
                    gathered[h, me] = share

                @pl.when(c != me)
                def _():
                    given[h, c] = share
                    give_copy(c, h).start()

    def layer_copy(k, h):
        q = above(k)
        return remote(
            gathered.at[h, pl.ds(q * tall, tall)], terms.at[h, layer],
            layer_send.at[h * layers + k], layer_recv.at[h * layers + layer], (q, me),
        )

    for h in range(CUTS):
        for k in range(1, parts):
            src = lax.rem(me + parts - k, parts)
            arrived(gathered.at[h, src], give_recv.at[h * parts + src])
        for k in range(1, layers):
            layer_copy(k, h).start()
        for a in range(tall):
            terms[h, layer, a] = gathered[h, layer * tall + a]

    my_tile, my_fold = lax.rem(me, per_fold), lax.div(me, per_fold)

    def piece_copy(f, h):
        return remote(
            sums.at[h, f], pieces.at[h, my_fold],
            piece_send.at[h * folds + f], piece_recv.at[h * folds + my_fold], (layer, my_tile + per_fold * f),
        )

    place = lax.broadcasted_iota(jnp.int32, (sub, tile), 1) + my_tile * tile
    for h in range(CUTS):
        for k in range(1, layers):
            src = lax.rem(layer + layers - k, layers)
            if h == 0:
                arrived(starts.at[src], start_recv.at[src])
            arrived(terms.at[h, src], layer_recv.at[h * layers + src])
        for f in range(folds):
            for a in range(tall):
                total = jnp.zeros((sub, tile), jnp.float32)
                for p in range(layers):
                    offset = place + f * points - starts[p][0:1, 0:1]
                    inside = (offset >= 0) & (offset < points)
                    total += jnp.where(inside, terms[h, p, a].astype(jnp.float32), 0.0)
                sums[h, f, a] = total.astype(jnp.bfloat16)

            @pl.when(my_fold == f)
            def _():
                pieces[h, f] = sums[h, f]

            @pl.when(my_fold != f)
            def _():
                piece_copy(f, h).start()

    for h in range(CUTS):
        for f in range(folds):

            @pl.when(my_fold != f)
            def _():
                arrived(pieces.at[h, f], piece_recv.at[h * folds + f])

            for a in range(tall):
                out[pl.ds(a * rows + h * cut + f * sub, sub), :] = pieces[h, f, a]

    for k in range(1, parts):
        for h in range(CUTS):
            image_copy(k, h).wait_send()
            row_copy(peer(k), h).wait_send()
            back_copy(k, h).wait_send()
            give_copy(peer(k), h).wait_send()
    for k in range(1, layers):
        start_copy(k).wait_send()
        for h in range(CUTS):
            layer_copy(k, h).wait_send()
    for f in range(folds):

        @pl.when(my_fold != f)
        def _():
            for h in range(CUTS):
                piece_copy(f, h).wait_send()


def strips(image, beam, counts, start, layers):
    points, wide = counts.shape
    rows, tile = beam.shape[0], image.shape[1]
    parts = points // rows
    folds = tile * parts // points
    coarse_cos, coarse_sin, fine_cos, fine_sin = (jnp.asarray(t) for t in make_tables(points))
    hp = max(wide // 2, 128)
    tall, sub = points // layers // rows, rows // CUTS // folds
    vmem, hbm = pl.BlockSpec(memory_space=pltpu.VMEM), pl.BlockSpec(memory_space=pl.ANY)
    bf = jnp.bfloat16
    dma = pltpu.SemaphoreType.DMA
    return pl.pallas_call(
        kernel,
        out_shape=jax.ShapeDtypeStruct((points // layers, tile), bf),
        in_specs=[hbm, hbm, hbm, vmem, hbm, hbm, vmem, vmem],
        out_specs=vmem,
        scratch_shapes=[
            pltpu.VMEM((2 * points, points), bf),
            pltpu.VMEM((points // 8, points), jnp.float32),
            pltpu.VMEM((points // 8, points), jnp.float32),
            pltpu.VMEM((rows, points), jnp.float32),
            pltpu.VMEM((points, wide), jnp.int32),
            pltpu.VMEM((parts, rows, tile), bf),
            pltpu.VMEM((rows, points), bf),
            pltpu.VMEM((parts, rows, wide), bf),
            pltpu.VMEM((points, wide), bf),
            pltpu.VMEM((2 * points, wide), bf),
            pltpu.VMEM((parts, rows, wide), bf),
            pltpu.VMEM((parts, rows, wide), bf),
            pltpu.VMEM((rows, points // 2), bf),
            pltpu.VMEM((rows, points // 2), bf),
            pltpu.VMEM((CUTS, parts, sub, tile), bf),
            pltpu.VMEM((CUTS, parts, sub, tile), bf),
            pltpu.VMEM((CUTS, layers, tall, sub, tile), bf),
            pltpu.VMEM((CUTS, folds, tall, sub, tile), bf),
            pltpu.VMEM((CUTS, folds, tall, sub, tile), bf),
            pltpu.VMEM((layers, 8, 128), jnp.int32),
            pltpu.VMEM((points, wide), bf),
            pltpu.VMEM((points, wide), bf),
            pltpu.VMEM((points, hp), bf),
            pltpu.VMEM((points, hp), bf),
            pltpu.VMEM((points, wide), bf),
            pltpu.VMEM((16, points), bf),
            pltpu.VMEM((16, points), bf),
            dma((4,)), dma(()), dma((CUTS * parts,)), dma((CUTS * parts,)), dma((CUTS * parts,)), dma((CUTS * parts,)),
            dma((CUTS * parts,)), dma((CUTS * parts,)), dma((CUTS * parts,)), dma((CUTS * parts,)),
            dma((CUTS * layers,)), dma((CUTS * layers,)),
            dma((layers,)), dma((layers,)), dma((CUTS * folds,)), dma((CUTS * folds,)), dma((4,)),
        ],
        compiler_params=pltpu.CompilerParams(
            collective_id=0, has_side_effects=True, vmem_limit_bytes=60 * 1024 * 1024
        ),
    )(image, beam, counts, start, coarse_cos, coarse_sin, fine_cos, fine_sin)


def shards(image, beam, counts, offsets):
    start = jnp.full((8, 128), offsets[0], jnp.int32)
    return strips(image, beam[0], counts[0], start, lax.axis_size("ptg")).astype(jnp.float32)


def solution(mesh):
    return jax.shard_map(
        shards,
        mesh=mesh,
        in_specs=(P(None, "img"), P("ptg", "img", None), P("ptg", None, "img"), P("ptg")),
        out_specs=P("ptg", "img"),
        check_vma=False,
    )
```
